128 devices in a mesh: group: 8 (over z, core), bulk: 16 (over x, y).
Axes of the slice: x: 4, y: 4, z: 4, core: 2. Of those that a mesh axis runs over, the one named last changes fastest.
Arguments:
- p_tiles: float32 [6144, 128, 128], P(('group', 'bulk')), may hold values from -0.5 to 0.5
- a_tiles: float32 [6144, 7, 128, 128], P(('group', 'bulk')), may hold values from -0.5 to 0.5
- col_ref: int32 [6144, 7], P(('group', 'bulk')), may hold values from 0 to 111, as said below
- send_list: int32 [128, 2, 32], P(('group', 'bulk')), may hold values from -1 to 47, as said below
- coarse_tile: int32 [6144, 7], P(('group', 'bulk')), may hold values from 0 to 127
Outputs:
- coarse_op: float32 [1024, 128, 128], P('group')
The draws below stay inside these ranges and needn't reach their ends.
Inputs may be any that keep to these rules, and one draw needn't show every extreme that they name: `send_list`: entry [s, 0, j] is the local index of a fine block of device s that device s - 1 receives in slot j, entry [s, 1, j] one that device s + 1 receives; the slots of one entry hold distinct blocks, filled slots come first, -1 marks an empty slot. Device 0 sends nothing below and the last device nothing above; every other pair fills between 16 and 32 slots, and device 0 fills all 32 slots for device 1. `col_ref`: on device d, a value v under 48 names d's own fine block v; a value v of 48 or more names the tile that d receives in slot (v - 48) % 32 from the slab below if (v - 48) // 32 is 0, from the slab above if it is 1, always a filled slot. Every filled slot that d receives is named by exactly one coupling of d.
All inputs are finite; a program needn't handle non-finite values.
Results may differ from the reference program's by a relative error of at most 0.0003.
Values sent between devices are 32-bit elements; how exact they have to be, the bound alone decides.
No kernel may reach another device: no remote copies, remote signals or barrier semaphores. Data moves between devices by JAX's collectives and lax.ppermute only.
A program may use at most 192 MiB of HBM per device.

```python
import jax
import jax.numpy as jnp
from jax import lax

BS = 128
CW = 128
K = 7
SCAP = 32
FB = 48
CT = 128
PEERS = 128
FINE = 6144
N_GROUP = 8
N_BULK = 16


def routing(key):
    count_key = jax.random.fold_in(key, 101)
    order_key = jax.random.fold_in(key, 102)
    counts = jax.random.randint(count_key, (PEERS, 2), SCAP // 2, SCAP + 1)
    sender = jnp.arange(PEERS)
    counts = counts.at[:, 0].set(jnp.where(sender == 0, 0, counts[:, 0]))
    counts = counts.at[:, 1].set(jnp.where(sender == PEERS - 1, 0, counts[:, 1]))
    counts = counts.at[0, 1].set(SCAP)
    scores = jax.random.randint(order_key, (PEERS, 2, FB), 0, 2 ** 20) * FB + jnp.arange(FB)
    order = jnp.argsort(scores, axis=-1)[:, :, :SCAP]
    slots = jnp.arange(SCAP)[None, None, :]
    sends = jnp.where(slots < counts[:, :, None], order, -1).astype(jnp.int32)
    return (counts, sends)


def draw_send_list(key, part):
    counts, sends = routing(key)
    return sends


def draw_col_ref(key, part):
    counts, sends = routing(key)
    key = jax.random.fold_in(key, 7)
    place_key = jax.random.fold_in(key, 1)
    local_key = jax.random.fold_in(key, 2)
    refs = 2 * SCAP
    places = FB * K
    zero = jnp.zeros((1,), counts.dtype)
    below = jnp.concatenate([zero, counts[:-1, 1]])
    above = jnp.concatenate([counts[1:, 0], zero])
    received = jnp.stack([below, above], axis=1)
    scores = jax.random.randint(place_key, (PEERS, places), 0, 2 ** 20) * places + jnp.arange(places)
    ranking = jnp.argsort(jnp.argsort(scores, axis=-1), axis=-1)
    live_table = (jnp.arange(SCAP)[None, None, :] < received[:, :, None]).reshape(PEERS, refs)
    picked = jnp.take_along_axis(live_table, jnp.minimum(ranking, refs - 1), axis=1)
    usable = (ranking < refs) & picked
    local = jax.random.randint(local_key, (PEERS, places), 0, FB)
    chosen = jnp.where(usable, FB + ranking, local)
    return chosen.reshape(PEERS * FB, K).astype(jnp.int32)


def plant(array, rng, least, high):
    extent = array.shape
    index_at = [jax.random.randint(jax.random.fold_in(rng, axis), (), 0, extent[axis]) for axis in range(len(extent))]
    array = array.at[tuple(index_at)].set(least)
    longest = extent.index(max(extent))
    index_at[longest] = (index_at[longest] + 1) % extent[longest]
    return array.at[tuple(index_at)].set(high)


def level_of(stream_key, dims, shards, smallest, high):
    def one(position, blocks):
        heights = jax.random.uniform(jax.random.fold_in(jax.random.fold_in(stream_key, 6), position), (blocks,), jnp.float32, smallest / len(shards), high / len(shards))
        return jnp.repeat(jnp.exp(heights), dims[position] // blocks).reshape((-1,) + (1,) * (len(dims) - position - 1))

    gain = one(*shards[0])
    for cut in shards[1:]:
        gain = gain * one(*cut)
    return gain


def gaussian(own_key, dims, width, limit, split=(), kind=jnp.bfloat16):
    gain = level_of(own_key, dims, split, -0.22, 0.18) if split else 1.0
    entries = jax.random.normal(own_key, dims, jnp.float32) * width * gain
    return jnp.minimum(jnp.maximum(entries, -limit), limit).astype(kind)


def setup_inputs(seed: int = 0) -> dict:
    key_of = jax.random.split(jax.random.key(seed), 6)
    return {
        "p_tiles": gaussian(key_of[0], (FINE, BS, CW), BS ** -0.5, 0.5, ((0, 128),), jnp.float32),
        "a_tiles": gaussian(key_of[1], (FINE, K, BS, BS), BS ** -0.5, 0.5, ((0, 128),), jnp.float32),
        "col_ref": draw_col_ref(jax.random.fold_in(key_of[5], 71), 0),
        "send_list": draw_send_list(jax.random.fold_in(key_of[5], 71), 0),
        "coarse_tile": plant(jax.random.randint(key_of[4], (FINE, K), 0, CT), jax.random.fold_in(key_of[4], 1), 0, CT - 1).astype(jnp.int32),
    }


def reference(p_tiles, a_tiles, col_ref, send_list, coarse_tile):
    owner = (jnp.arange(PEERS * FB, dtype=jnp.int32) // FB)[:, None]
    owner = jnp.broadcast_to(owner, col_ref.shape)
    remote = col_ref - FB
    side = jnp.clip(remote // SCAP, 0, 1).astype(jnp.int32)
    slot_index = jnp.clip(remote % SCAP, 0, SCAP - 1).astype(jnp.int32)
    source = jnp.clip(owner + 2 * side - 1, 0, PEERS - 1).astype(jnp.int32)
    sent_block = send_list[source, (1 - side).astype(jnp.int32), slot_index]
    global_col = jnp.where(col_ref < FB, owner * FB + col_ref, source * FB + jnp.maximum(sent_block, 0)).astype(jnp.int32)

    def one_device(device):
        start = (device * FB).astype(jnp.int32)
        row_tiles = lax.dynamic_slice_in_dim(p_tiles, start, FB, 0)
        couplings = lax.dynamic_slice_in_dim(a_tiles, start, FB, 0).reshape(FB * K, BS, BS)
        col_index = lax.dynamic_slice_in_dim(global_col, start, FB, 0).reshape(-1)
        targets = lax.dynamic_slice_in_dim(coarse_tile, start, FB, 0).reshape(-1)
        right_tiles = p_tiles[col_index]
        product = jnp.einsum("qxy,qyc->qxc", couplings, right_tiles, precision=lax.Precision.HIGHEST)
        triple = jnp.einsum("ixa,ikxc->ikac", row_tiles, product.reshape(FB, K, BS, CW), precision=lax.Precision.HIGHEST)
        return jax.ops.segment_sum(triple.reshape(FB * K, CW, CW), targets, num_segments=CT)

    def group_sum(group_index):
        def add_slab(running, bulk_index):
            return running + one_device(group_index * N_BULK + bulk_index), None

        running, _ = lax.scan(add_slab, jnp.zeros((CT, CW, CW), jnp.float32), jnp.arange(N_BULK, dtype=jnp.int32))
        return running

    result = lax.map(group_sum, jnp.arange(N_GROUP, dtype=jnp.int32))
    return result.reshape(N_GROUP * CT, CW, CW)
```

```python
import functools

import jax
import jax.numpy as jnp
from jax import lax
from jax.experimental import pallas as pl
from jax.experimental.pallas import tpu as pltpu
from jax.sharding import PartitionSpec as P

F32 = jnp.float32
BF16 = jnp.bfloat16
SIDE = 4
MB = 1 << 20


def parts_of(x):
    high = x.astype(BF16)
    return high, (x - high.astype(F32)).astype(BF16)


def row_pair(x):
    return jnp.concatenate(parts_of(x), axis=1)


def column_pair(x):
    pair = row_pair(x)
    return jnp.concatenate([pair, pair], axis=0)


def fold(x):
    n = x.shape[1] // 2
    return x[:, :n] + x[:, n:]


def product(left_pair, right_pair):
    return fold(jnp.dot(left_pair, right_pair, preferred_element_type=F32))


def choose_kernel(send_ref, p_ref, low_ref, up_ref, held, sem):
    capacity = send_ref.shape[1]
    outs = ((0, low_ref), (1, up_ref))
    load = pltpu.make_async_copy(p_ref, held, sem.at[2])
    load.start()
    load.wait()

    @pl.loop(0, capacity)
    def _(j):
        for side, out in outs:
            tile = jnp.maximum(send_ref[side, j], 0)
            pltpu.make_async_copy(held.at[tile], out.at[j], sem.at[side]).start()

    for side, out in outs:
        pltpu.make_async_copy(held.at[pl.ds(0, capacity)], out, sem.at[side]).wait()


def choose(send, p_tiles):
    capacity = send.shape[1]
    tile = p_tiles.shape[1:]
    out = jax.ShapeDtypeStruct((capacity,) + tile, F32)
    return pl.pallas_call(
        choose_kernel,
        name="choose",
        out_shape=(out, out),
        in_specs=[pl.BlockSpec(memory_space=pltpu.SMEM), pl.BlockSpec(memory_space=pl.ANY)],
        out_specs=(pl.BlockSpec(memory_space=pl.ANY),) * 2,
        scratch_shapes=[pltpu.VMEM(p_tiles.shape, F32), pltpu.SemaphoreType.DMA((3,))],
        compiler_params=pltpu.CompilerParams(vmem_limit_bytes=16 * MB),
        cost_estimate=pl.CostEstimate(flops=0, bytes_accessed=4 * 32 * 65536, transcendentals=0),
    )(send, p_tiles)


BLOCKS = 4


def local_kernel(col_ref, target_ref, p_ref, a_ref, part_ref, left_ref, slot_ref, packed, total, left, sem):
    step = pl.program_id(0)
    blocks = p_ref.shape[0]
    slots = left_ref.shape[0] - 1
    spare = total.shape[0] - 1

    @pl.when(step == 0)
    def _():
        @pl.loop(0, blocks)
        def _(i):
            packed[i] = column_pair(p_ref[i])

        @pl.loop(0, spare + 1)
        def _(i):
            total[i] = jnp.zeros(total.shape[1:], F32)

        @pl.loop(0, slots)
        def _(i):
            slot_ref[i] = -1

    neighbours = a_ref.shape[1]
    for i in range(BLOCKS):
        f = step * BLOCKS + i
        rows = row_pair(p_ref[f].T)
        places = []
        for k in range(neighbours):
            v = col_ref[f * neighbours + k]
            t = target_ref[f * neighbours + k]
            remote = v >= blocks
            slot = jnp.where(remote, v - blocks, slots)
            slot_ref[slot] = t
            places.append((slot, jnp.where(remote, 0, v), jnp.where(remote, spare, t)))
        lefts = [product(rows, column_pair(a_ref[i, k])) for k in range(neighbours)]
        for w, (slot, _, _) in zip(lefts, places):
            left[slot] = w
        terms = [product(row_pair(w), packed[q]) for w, (_, q, _) in zip(lefts, places)]
        for term, (_, _, t) in zip(terms, places):
            total[t] += term

    @pl.when(step == pl.num_programs(0) - 1)
    def _():
        one = pltpu.make_async_copy(total, part_ref, sem.at[0])
        two = pltpu.make_async_copy(left, left_ref, sem.at[1])
        one.start()
        two.start()
        one.wait()
        two.wait()


def local_part(col, target, p_tiles, a_tiles, tiles, slots):
    blocks, bs, cw = p_tiles.shape
    neighbours = a_tiles.shape[1]
    part = jax.ShapeDtypeStruct((tiles + 1, cw, cw), F32)
    left = jax.ShapeDtypeStruct((slots + 1, cw, bs), F32)
    return pl.pallas_call(
        local_kernel,
        name="local_part",
        grid_spec=pltpu.PrefetchScalarGridSpec(
            num_scalar_prefetch=2,
            grid=(blocks // BLOCKS,),
            in_specs=[
                pl.BlockSpec((blocks, bs, cw), lambda f, *_: (0, 0, 0)),
                pl.BlockSpec((BLOCKS, neighbours, bs, bs), lambda f, *_: (f, 0, 0, 0)),
            ],
            out_specs=(
                pl.BlockSpec(memory_space=pl.ANY),
                pl.BlockSpec(memory_space=pl.ANY),
                pl.BlockSpec(memory_space=pltpu.SMEM),
            ),
            scratch_shapes=[
                pltpu.VMEM((blocks, 2 * bs, 2 * cw), BF16),
                pltpu.VMEM(part.shape, F32),
                pltpu.VMEM(left.shape, F32),
                pltpu.SemaphoreType.DMA((2,)),
            ],
        ),
        out_shape=(part, left, jax.ShapeDtypeStruct((slots + 8,), jnp.int32)),
        compiler_params=pltpu.CompilerParams(vmem_limit_bytes=44 * MB),
        cost_estimate=pl.CostEstimate(flops=24 * 10**9, bytes_accessed=36 * 10**6, transcendentals=0),
    )(col, target, p_tiles, a_tiles)


GROUP = 4


def remote_kernel(chunks, slot_ref, left_ref, lower_ref, upper_ref, part_ref, *rest):
    outs, (todo, total, held_left, held_right, sem, io_sem) = rest[: len(chunks)], rest[len(chunks) :]
    size = outs[0].shape[0]
    capacity = lower_ref.shape[0]
    spare = len(chunks) * size
    places = 2 * capacity + GROUP
    loads = [
        pltpu.make_async_copy(part_ref.at[pl.ds(c, size)], total.at[pl.ds(i * size, size)], io_sem.at[i])
        for i, c in enumerate(chunks)
    ]
    for load in loads:
        load.start()

    def find(j, n):
        t = slot_ref[j]
        place = jnp.int32(-1)
        for i, c in enumerate(chunks):
            place = jnp.where((t >= c) & (t < c + size), t - c + i * size, place)
        todo[n] = j
        todo[n + places] = place
        return n + (place >= 0).astype(jnp.int32)

    count = lax.fori_loop(0, 2 * capacity, find, jnp.int32(0))
    for i in range(GROUP):
        todo[count + i] = 0
        todo[count + i + places] = spare
    groups = (count + GROUP - 1) // GROUP

    def start(g):
        b = lax.rem(g, 2)
        for i in range(GROUP):
            j = todo[g * GROUP + i]
            pltpu.make_async_copy(left_ref.at[j], held_left.at[b, i], sem.at[0, b]).start()

            @pl.when(j < capacity)
            def _():
                pltpu.make_async_copy(lower_ref.at[j], held_right.at[b, i], sem.at[1, b]).start()

            @pl.when(j >= capacity)
            def _():
                pltpu.make_async_copy(upper_ref.at[j - capacity], held_right.at[b, i], sem.at[1, b]).start()

    @pl.when(groups > 0)
    def _():
        start(jnp.int32(0))

    for load in loads:
        load.wait()

    def step(g, carry):
        @pl.when(g + 1 < groups)
        def _():
            start(g + 1)

        b = lax.rem(g, 2)
        pltpu.make_async_copy(left_ref.at[pl.ds(0, GROUP)], held_left.at[b], sem.at[0, b]).wait()
        pltpu.make_async_copy(lower_ref.at[pl.ds(0, GROUP)], held_right.at[b], sem.at[1, b]).wait()
        terms = [product(row_pair(held_left[b, i]), column_pair(held_right[b, i])) for i in range(GROUP)]
        for i, term in enumerate(terms):
            total[todo[g * GROUP + i + places]] += term
        return carry

    lax.fori_loop(0, groups, step, 0)
    stores = [
        pltpu.make_async_copy(total.at[pl.ds(i * size, size)], out, io_sem.at[i]) for i, out in enumerate(outs)
    ]
    for store in stores:
        store.start()
    for store in stores:
        store.wait()


def remote_part(chunks, size, slots, left, lower, upper, part):
    tile = part.shape[1:]
    out = jax.ShapeDtypeStruct((size,) + tile, F32)
    n = len(chunks)
    anywhere = pl.BlockSpec(memory_space=pl.ANY)
    return pl.pallas_call(
        functools.partial(remote_kernel, chunks),
        name="remote_part",
        out_shape=(out,) * n,
        in_specs=[pl.BlockSpec(memory_space=pltpu.SMEM)] + [anywhere] * 4,
        out_specs=(anywhere,) * n,
        scratch_shapes=[
            pltpu.SMEM((4 * lower.shape[0] + 2 * GROUP,), jnp.int32),
            pltpu.VMEM((n * size + 1,) + tile, F32),
            pltpu.VMEM((2, GROUP) + tile, F32),
            pltpu.VMEM((2, GROUP) + tile, F32),
            pltpu.SemaphoreType.DMA((2, 2)),
            pltpu.SemaphoreType.DMA((n,)),
        ],
        compiler_params=pltpu.CompilerParams(vmem_limit_bytes=16 * MB),
        cost_estimate=pl.CostEstimate(flops=10**9, bytes_accessed=2 * n * size * 65536, transcendentals=0),
    )(slots, left, lower, upper, part)


def place_kernel(pieces, *refs):
    n = len(pieces)
    ins = refs[:n]
    out_ref, held, load_sem, store_sem = refs[-4:]
    at = lax.axis_index("bulk")
    x, y = at // SIDE, lax.rem(at, SIDE)
    quarter = 4
    loads, stores = [], []
    first = 0
    for ref, entries in zip(ins, pieces):
        loads.append(pltpu.make_async_copy(ref, held.at[pl.ds(first, ref.shape[0])], load_sem.at[len(loads)]))
        for i, (half, dx, dy) in enumerate(entries):
            where = half * 64 + lax.rem(x + dx, SIDE) * 16 + lax.rem(y + dy, SIDE) * quarter
            stores.append(
                pltpu.make_async_copy(
                    held.at[pl.ds(first + i * quarter, quarter)],
                    out_ref.at[pl.ds(where, quarter)],
                    store_sem.at[len(stores)],
                )
            )
        first += ref.shape[0]
    for load in loads:
        load.start()
    started = 0
    for load, entries in zip(loads, pieces):
        load.wait()
        for store in stores[started : started + len(entries)]:
            store.start()
        started += len(entries)
    for store in stores:
        store.wait()


def place(arrays, pieces, shape, out=None):
    anywhere = pl.BlockSpec(memory_space=pl.ANY)
    count = sum(len(entries) for entries in pieces)
    args = list(arrays) + ([] if out is None else [out])
    return pl.pallas_call(
        functools.partial(place_kernel, pieces),
        name="place",
        out_shape=jax.ShapeDtypeStruct(shape, F32),
        in_specs=[anywhere] * len(args),
        out_specs=anywhere,
        scratch_shapes=[
            pltpu.VMEM((count * 4,) + shape[1:], F32),
            pltpu.SemaphoreType.DMA((len(arrays),)),
            pltpu.SemaphoreType.DMA((count,)),
        ],
        compiler_params=pltpu.CompilerParams(vmem_limit_bytes=16 * MB),
        input_output_aliases={} if out is None else {len(arrays): 0},
        cost_estimate=pl.CostEstimate(flops=0, bytes_accessed=2 * count * 4 * 65536, transcendentals=0),
    )(*args)


def route(dx, dy):
    pairs = []
    for x in range(SIDE):
        for y in range(SIDE):
            pairs.append((x * SIDE + y, (x + dx) % SIDE * SIDE + (y + dy) % SIDE))
    return pairs


def push(block, axis, distance):
    dx, dy = (distance, 0) if axis == "x" else (0, distance)
    return lax.ppermute(block, "bulk", route(dx, dy))


def shifted(block, axis, distance):
    devices = range(lax.axis_size(axis))
    pairs = [(i - distance, i) for i in devices if i - distance in devices]
    return lax.ppermute(block, axis, pairs)


def shards(p_tiles, a_tiles, col_ref, send_list, coarse_tile):
    tiles = 128
    slots = 2 * send_list.shape[2]
    at = lax.axis_index("bulk")
    x, y = at // SIDE, at % SIDE
    second = coarse_tile // 64
    ahead_x = (coarse_tile // 16 - x) % SIDE
    ahead_y = (coarse_tile // 4 - y) % SIDE
    outer = jnp.where(second == 0, ahead_x, ahead_y)
    inner = jnp.where(second == 0, ahead_y, ahead_x)
    target = second * 64 + outer * 16 + inner * 4 + coarse_tile % 4

    to_lower, to_upper = choose(send_list[0], p_tiles)
    lower = shifted(to_upper, ("group", "bulk"), 1)
    upper = shifted(to_lower, ("group", "bulk"), -1)
    part, left, slot_tile = local_part(
        col_ref.reshape(-1), target.reshape(-1), p_tiles, a_tiles, tiles, slots
    )
    more = (slot_tile, left, lower, upper, part)
    far = remote_part((32, 40, 96, 104), 8, *more)
    near = remote_part((16, 24, 48, 56, 80, 88, 112, 120), 8, *more)
    here = remote_part((0, 8, 64, 72), 8, *more)

    axes = (("x", "y"), ("y", "x"))
    owned = []
    for half, (outer_axis, _) in enumerate(axes):
        far_a, far_b = far[2 * half : 2 * half + 2]
        up_a, up_b, down_a, down_b = near[4 * half : 4 * half + 4]
        here_a, here_b = here[2 * half : 2 * half + 2]
        first_up = push(far_a, outer_axis, 1)
        first_down = push(far_b, outer_axis, -1)
        second_up = push(up_b, outer_axis, 1)
        second_down = push(down_a, outer_axis, -1)
        third_up = push(up_a + first_up, outer_axis, 1)
        third_down = push(down_b + first_down, outer_axis, -1)
        owned.append((here_a + second_down + third_up, here_b + second_up + third_down))
    sums = []
    for half, (_, inner_axis) in enumerate(axes):
        one, two = owned[half]
        next_up = push(one[4:], inner_axis, 1)
        opposite = push(two[:4], inner_axis, 2)
        next_down = push(two[4:], inner_axis, -1)
        sums.append(one[:4] + next_up + opposite + next_down)
    gathered = []
    for half, (_, inner_axis) in enumerate(axes):
        own = sums[half]
        behind = push(own, inner_axis, 1)
        ahead = push(own, inner_axis, -1)
        opposite = push(own, inner_axis, 2)
        gathered.append((jnp.concatenate([own, ahead]), jnp.concatenate([opposite, behind])))
    early, early_pieces, late, late_pieces = [], [], [], []

    def entry(half, outer, inner):
        return (half, outer, inner) if half == 0 else (half, inner, outer)

    for half, (outer_axis, _) in enumerate(axes):
        one, two = gathered[half]
        behind_one = push(one, outer_axis, 1)
        ahead_two = push(two, outer_axis, -1)
        behind_two = push(two, outer_axis, 1)
        ahead_one = push(one, outer_axis, -1)
        far_one = push(behind_one, outer_axis, 1)
        far_two = push(ahead_two, outer_axis, -1)
        for arr, outer, inners in (
            (one, 0, (0, 1)),
            (two, 0, (2, 3)),
            (behind_one, 3, (0, 1)),
            (behind_two, 3, (2, 3)),
            (ahead_one, 1, (0, 1)),
            (ahead_two, 1, (2, 3)),
        ):
            early.append(arr)
            early_pieces.append([entry(half, outer, i) for i in inners])
        for arr, inners in ((far_one, (0, 1)), (far_two, (2, 3))):
            late.append(arr)
            late_pieces.append([entry(half, 2, i) for i in inners])
    shape = (tiles,) + p_tiles.shape[2:] * 2
    out = place(early, early_pieces, shape)
    return place(late, late_pieces, shape, out)


def solution(mesh):
    in_specs = (
        P(("group", "bulk"), None, None),
        P(("group", "bulk"), None, None, None),
        P(("group", "bulk"), None),
        P(("group", "bulk"), None, None),
        P(("group", "bulk"), None),
    )
    out_specs = P("group", None, None)
    return jax.shard_map(shards, mesh=mesh, in_specs=in_specs, out_specs=out_specs, check_vma=False)
```

```python
import functools

import jax
import jax.numpy as jnp
from jax import lax
from jax.experimental import pallas as pl
from jax.experimental.pallas import tpu as pltpu
from jax.sharding import PartitionSpec as P

F32 = jnp.float32
BF16 = jnp.bfloat16
SIDE = 4
MB = 1 << 20


def parts_of(x):
    high = x.astype(BF16)
    return high, (x - high.astype(F32)).astype(BF16)


def row_pair(x):
    return jnp.concatenate(parts_of(x), axis=1)


def column_pair(x):
    pair = row_pair(x)
    return jnp.concatenate([pair, pair], axis=0)


def fold(x):
    n = x.shape[1] // 2
    return x[:, :n] + x[:, n:]


def product(left_pair, right_pair):
    return fold(jnp.dot(left_pair, right_pair, preferred_element_type=F32))


def choose_kernel(send_ref, p_ref, *rest):
    outs, (held, load_sem, sem) = rest[:-3], rest[-3:]
    load = pltpu.make_async_copy(p_ref, held, load_sem)
    load.start()
    load.wait()
    for i, out in enumerate(outs):
        side, first = i % 2, sum(outs[j].shape[0] for j in range(i % 2, i, 2))

        @pl.loop(0, out.shape[0])
        def _(j):
            tile = jnp.maximum(send_ref[side, first + j], 0)
            pltpu.make_async_copy(held.at[tile], out.at[j], sem.at[i]).start()

    for i, out in enumerate(outs):
        pltpu.make_async_copy(held.at[pl.ds(0, out.shape[0])], out, sem.at[i]).wait()


def choose(send, p_tiles, sizes):
    tile = p_tiles.shape[1:]
    out = tuple(jax.ShapeDtypeStruct((size,) + tile, F32) for size in sizes for _ in range(2))
    return pl.pallas_call(
        choose_kernel,
        name="choose",
        out_shape=out,
        in_specs=[pl.BlockSpec(memory_space=pltpu.SMEM), pl.BlockSpec(memory_space=pltpu.HBM)],
        out_specs=(pl.BlockSpec(memory_space=pl.ANY),) * len(out),
        scratch_shapes=[
            pltpu.VMEM(p_tiles.shape, F32),
            pltpu.SemaphoreType.DMA,
            pltpu.SemaphoreType.DMA((len(out),)),
        ],
        compiler_params=pltpu.CompilerParams(vmem_limit_bytes=16 * MB),
        cost_estimate=pl.CostEstimate(flops=0, bytes_accessed=4 * 32 * 65536, transcendentals=0),
    )(send, p_tiles)


BLOCKS = 4


def local_kernel(
    col_ref, target_ref, p_hbm, a_ref, *refs
):
    part_refs, (left_ref, slot_ref, p_ref, packed, total, left, sem) = refs[:-7], refs[-7:]
    step = pl.program_id(0)
    blocks = p_ref.shape[0]
    slots = left_ref.shape[0] - 1
    spare = total.shape[0] - 1

    @pl.when(step == 0)
    def _():
        load = pltpu.make_async_copy(p_hbm, p_ref, sem.at[0])
        load.start()
        load.wait()

        @pl.loop(0, blocks)
        def _(i):
            packed[i] = column_pair(p_ref[i])

        @pl.loop(0, spare + 1)
        def _(i):
            total[i] = jnp.zeros(total.shape[1:], F32)

        @pl.loop(0, slots)
        def _(i):
            slot_ref[i] = -1

    neighbours = a_ref.shape[1]
    for i in range(BLOCKS):
        f = step * BLOCKS + i
        rows = row_pair(p_ref[f].T)
        places = []
        for k in range(neighbours):
            v = col_ref[f * neighbours + k]
            t = target_ref[f * neighbours + k]
            remote = v >= blocks
            slot = jnp.where(remote, v - blocks, slots)
            slot_ref[slot] = t
            places.append((slot, jnp.where(remote, 0, v), jnp.where(remote, spare, t)))
        lefts = [product(rows, column_pair(a_ref[i, k])) for k in range(neighbours)]
        for w, (slot, _, _) in zip(lefts, places):
            left[slot] = w
        terms = [product(row_pair(w), packed[q]) for w, (_, q, _) in zip(lefts, places)]
        for term, (_, _, t) in zip(terms, places):
            total[t] += term

    @pl.when(step == pl.num_programs(0) - 1)
    def _():
        stores = [pltpu.make_async_copy(left, left_ref, sem.at[len(part_refs)])]
        first = 0
        for i, part in enumerate(part_refs):
            stores.append(pltpu.make_async_copy(total.at[pl.ds(first, part.shape[0])], part, sem.at[i]))
            first += part.shape[0]
        for store in stores:
            store.start()
        for store in stores:
            store.wait()


def local_part(col, target, p_tiles, a_tiles, sizes, slots):
    blocks, bs, cw = p_tiles.shape
    neighbours = a_tiles.shape[1]
    parts = tuple(jax.ShapeDtypeStruct((size, cw, cw), F32) for size in sizes)
    left = jax.ShapeDtypeStruct((slots + 1, cw, bs), F32)
    return pl.pallas_call(
        local_kernel,
        name="local_part",
        grid_spec=pltpu.PrefetchScalarGridSpec(
            num_scalar_prefetch=2,
            grid=(blocks // BLOCKS,),
            in_specs=[
                pl.BlockSpec(memory_space=pltpu.HBM),
                pl.BlockSpec((BLOCKS, neighbours, bs, bs), lambda f, *_: (f, 0, 0, 0)),
            ],
            out_specs=(pl.BlockSpec(memory_space=pl.ANY),) * (len(parts) + 1)
            + (pl.BlockSpec(memory_space=pltpu.SMEM),),
            scratch_shapes=[
                pltpu.VMEM(p_tiles.shape, F32),
                pltpu.VMEM((blocks, 2 * bs, 2 * cw), BF16),
                pltpu.VMEM((sum(sizes) + 1, cw, cw), F32),
                pltpu.VMEM(left.shape, F32),
                pltpu.SemaphoreType.DMA((len(parts) + 1,)),
            ],
        ),
        out_shape=parts + (left, jax.ShapeDtypeStruct((slots + 8,), jnp.int32)),
        compiler_params=pltpu.CompilerParams(vmem_limit_bytes=28 * MB),
        cost_estimate=pl.CostEstimate(flops=10**9, bytes_accessed=10**7, transcendentals=0),
    )(col, target, p_tiles, a_tiles)


GROUP = 4


def remote_kernel(first, base, slot_ref, left_ref, lower_ref, upper_ref, *refs):
    parts, todo = refs[len(refs) // 2 : -1], refs[-1]
    capacity = lower_ref.shape[0]
    slots = (left_ref.shape[0] - 1) // 2
    places = 2 * capacity + GROUP
    held = sum(part.shape[0] for part in parts)

    def find(j, n):
        place = slot_ref[jnp.where(j < capacity, base + j, slots + base + j - capacity)] - first
        wanted = (place >= 0) & (place < held)
        todo[n] = j
        todo[n + places] = place
        return n + wanted.astype(jnp.int32)

    count = lax.fori_loop(0, 2 * capacity, find, jnp.int32(0))
    for i in range(GROUP):
        todo[count + i] = 0
        todo[count + i + places] = -1

    def step(g, carry):
        terms = []
        for i in range(GROUP):
            j = todo[g * GROUP + i]
            above = j >= capacity
            k = jnp.where(above, j - capacity, j)
            received = jnp.where(above, upper_ref[k], lower_ref[k])
            terms.append(product(row_pair(left_ref[base + k + jnp.where(above, slots, 0)]), column_pair(received)))
        for i, term in enumerate(terms):
            place = todo[g * GROUP + i + places]
            start = 0
            for part in parts:
                here = place - start

                @pl.when((here >= 0) & (here < part.shape[0]))
                def _():
                    part[here] += term

                start += part.shape[0]
        return carry

    lax.fori_loop(0, (count + GROUP - 1) // GROUP, step, 0)


def remote_part(first, base, slots, left, lower, upper, parts):
    n = len(parts)
    vmem = pl.BlockSpec(memory_space=pltpu.VMEM)
    return pl.pallas_call(
        functools.partial(remote_kernel, first, base),
        name="remote_part",
        out_shape=tuple(jax.ShapeDtypeStruct(part.shape, F32) for part in parts),
        in_specs=[pl.BlockSpec(memory_space=pltpu.SMEM)] + [vmem] * (3 + n),
        out_specs=(vmem,) * n,
        scratch_shapes=[pltpu.SMEM((4 * lower.shape[0] + 2 * GROUP,), jnp.int32)],
        input_output_aliases={4 + i: i for i in range(n)},
        compiler_params=pltpu.CompilerParams(vmem_limit_bytes=24 * MB),
        cost_estimate=pl.CostEstimate(flops=10**8, bytes_accessed=10**6, transcendentals=0),
    )(slots, left, lower, upper, *parts)


def place_kernel(pieces, *refs):
    n = len(pieces)
    ins = refs[:n]
    out_ref, held, load_sem, store_sem = refs[-4:]
    at = lax.axis_index("bulk")
    x, y = at // SIDE, lax.rem(at, SIDE)
    loads, stores = [], []
    first = 0
    for ref, entries in zip(ins, pieces):
        loads.append(pltpu.make_async_copy(ref, held.at[pl.ds(first, ref.shape[0])], load_sem.at[len(loads)]))
        for where, size, ox, oy, h in entries:
            ox, oy = (lax.rem(x + ox, SIDE), oy) if h == 0 else (ox, lax.rem(y + oy, SIDE))
            where = where + (ox * SIDE + oy) * size
            stores.append(
                pltpu.make_async_copy(
                    held.at[pl.ds(first, size)], out_ref.at[pl.ds(where, size)], store_sem.at[len(stores)]
                )
            )
            first += size
    for load in loads:
        load.start()
    started = 0
    for load, entries in zip(loads, pieces):
        load.wait()
        for store in stores[started : started + len(entries)]:
            store.start()
        started += len(entries)
    for store in stores:
        store.wait()


def place(arrays, pieces, shape, out=None):
    anywhere = pl.BlockSpec(memory_space=pl.ANY)
    hbm = pl.BlockSpec(memory_space=pltpu.HBM)
    count = sum(len(entries) for entries in pieces)
    held = sum(array.shape[0] for array in arrays)
    args = list(arrays) + ([] if out is None else [out])
    return pl.pallas_call(
        functools.partial(place_kernel, pieces),
        name="place",
        out_shape=jax.ShapeDtypeStruct(shape, F32),
        in_specs=[anywhere] * len(arrays) + [hbm] * (len(args) - len(arrays)),
        out_specs=hbm,
        scratch_shapes=[
            pltpu.VMEM((held,) + shape[1:], F32),
            pltpu.SemaphoreType.DMA((len(arrays),)),
            pltpu.SemaphoreType.DMA((count,)),
        ],
        compiler_params=pltpu.CompilerParams(vmem_limit_bytes=16 * MB),
        input_output_aliases={} if out is None else {len(arrays): 0},
        cost_estimate=pl.CostEstimate(flops=0, bytes_accessed=2 * held * 65536, transcendentals=0),
    )(*args)


def route(dx, dy):
    pairs = []
    for x in range(SIDE):
        for y in range(SIDE):
            pairs.append((x * SIDE + y, (x + dx) % SIDE * SIDE + (y + dy) % SIDE))
    return pairs


def push(block, axis, distance):
    dx, dy = (distance, 0) if axis == "x" else (0, distance)
    return lax.ppermute(block, "bulk", route(dx, dy))


def swap(block, axis, odd):
    pairs = []
    for x in range(SIDE):
        for y in range(SIDE):
            to = [x, y]
            i = 0 if axis == "x" else 1
            to[i] = ((to[i] + odd) % SIDE ^ 1) - odd
            pairs.append((x * SIDE + y, to[0] % SIDE * SIDE + to[1] % SIDE))
    return lax.ppermute(block, "bulk", pairs)


def shifted(block, axis, distance):
    devices = range(lax.axis_size(axis))
    pairs = [(i - distance, i) for i in devices if i - distance in devices]
    return lax.ppermute(block, axis, pairs)


FIRST = 16
EIGHTHS = (6, 7, 4, 1, 0, 2, 3, 5)


def shards(p_tiles, a_tiles, col_ref, send_list, coarse_tile):
    tiles = 128
    size = tiles // 2 // (SIDE * SIDE)
    eighth = 2 * size
    capacity = send_list.shape[2]
    at = lax.axis_index("bulk")
    x, y = at // SIDE, at % SIDE
    half = coarse_tile // (tiles // 2)
    owner = coarse_tile // size
    ahead_x, ahead_y = (owner // SIDE - x) % SIDE, (owner - y) % SIDE
    outer = jnp.where(half == 0, ahead_x, ahead_y)
    inner = jnp.where(half == 0, owner % SIDE, owner // SIDE % SIDE)
    key = outer * 2 + inner // 2
    where = sum(jnp.where(key == i, at_eighth, 0) for i, at_eighth in enumerate(EIGHTHS))
    target = ((where // 4 * 2 + half) * 4 + where % 4) * eighth + inner % 2 * size + coarse_tile % size

    sizes = (FIRST, capacity - FIRST)
    halo = []
    sent = choose(send_list[0], p_tiles, sizes)
    for i in range(len(sizes)):
        lower = shifted(sent[2 * i + 1], ("group", "bulk"), 1)
        upper = shifted(sent[2 * i], ("group", "bulk"), -1)
        halo.append((lower, upper))
    mid = tiles // 2
    early_sizes = [n * eighth for n in (2, 2, 2, 2)]
    late_sizes = [n * eighth for n in (1, 1, 2, 1, 1, 2)]
    *parts, left, slot_tile = local_part(
        col_ref.reshape(-1), target.reshape(-1), p_tiles, a_tiles, early_sizes + late_sizes, 2 * capacity
    )
    early, late = parts[: len(early_sizes)], parts[len(early_sizes) :]
    early = remote_part(0, 0, slot_tile, left, *halo[0], early)
    late = remote_part(mid, 0, slot_tile, left, *halo[0], late)
    firsts = remote_part(0, FIRST, slot_tile, left, *halo[1], early)
    rests = remote_part(mid, FIRST, slot_tile, left, *halo[1], late)

    axes = (("x", "y"), ("y", "x"))
    owned = []
    arrived = [
        (push(firsts[2 * h], axis, 1), push(firsts[2 * h + 1], axis, -1)) for h, (axis, _) in enumerate(axes)
    ]
    for h, (axis, _) in enumerate(axes):
        up, down, kept = rests[3 * h : 3 * h + 3]
        from_below, from_above = arrived[h]
        up = push(up + from_below[:eighth], axis, 1)
        down = push(down + from_above[:eighth], axis, -1)
        owned.append((kept[:eighth] + from_above[eighth:] + up, kept[eighth:] + from_below[eighth:] + down))
    gathered = []
    for h, (_, axis) in enumerate(axes):
        one, two = owned[h]
        one, two = one + swap(one, axis, 0), two + swap(two, axis, 1)
        one, two = one + swap(one, axis, 1), two + swap(two, axis, 0)
        gathered.append(jnp.concatenate([one, two]))
    first, first_pieces, last, last_pieces = [], [], [], []

    def entry(h, outer, inner):
        return (h * mid, size) + ((outer, inner) if h == 0 else (inner, outer)) + (h,)

    for h, (axis, _) in enumerate(axes):
        behind = push(gathered[h], axis, 1)
        ahead = push(gathered[h], axis, -1)
        far_one = push(behind[:eighth], axis, 1)
        far_two = push(ahead[eighth:], axis, -1)
        for array, outer in ((gathered[h], 0), (behind, 3), (ahead, 1)):
            first.append(array)
            first_pieces.append([entry(h, outer, i) for i in range(SIDE)])
        for array, inners in ((far_one, (0, 1)), (far_two, (2, 3))):
            last.append(array)
            last_pieces.append([entry(h, 2, i) for i in inners])
    shape = (tiles,) + p_tiles.shape[2:] * 2
    out = place(first, first_pieces, shape)
    return place(last, last_pieces, shape, out)


def solution(mesh):
    in_specs = (
        P(("group", "bulk"), None, None),
        P(("group", "bulk"), None, None, None),
        P(("group", "bulk"), None),
        P(("group", "bulk"), None, None),
        P(("group", "bulk"), None),
    )
    out_specs = P("group", None, None)
    return jax.shard_map(shards, mesh=mesh, in_specs=in_specs, out_specs=out_specs, check_vma=False)
```

```python
import functools

import jax
import jax.numpy as jnp
from jax import lax
from jax.experimental import pallas as pl
from jax.experimental.pallas import tpu as pltpu
from jax.sharding import PartitionSpec as P

F32 = jnp.float32
BF16 = jnp.bfloat16
SIDE = 4
MB = 1 << 20


def parts_of(x):
    high = x.astype(BF16)
    return high, (x - high.astype(F32)).astype(BF16)


def row_pair(x):
    return jnp.concatenate(parts_of(x), axis=1)


def column_pair(x):
    pair = row_pair(x)
    return jnp.concatenate([pair, pair], axis=0)


def fold(x):
    n = x.shape[1] // 2
    return x[:, :n] + x[:, n:]


def product(left_pair, right_pair):
    return fold(jnp.dot(left_pair, right_pair, preferred_element_type=F32))


def choose_kernel(first, send_ref, p_ref, low_ref, up_ref):
    for j in range(low_ref.shape[0]):
        for side, out in enumerate((low_ref, up_ref)):
            out[j] = p_ref[jnp.maximum(send_ref[side, first + j], 0)]


def choose(send, p_tiles, first, size):
    out = jax.ShapeDtypeStruct((size,) + p_tiles.shape[1:], F32)
    vmem = pl.BlockSpec(memory_space=pltpu.VMEM)
    return pl.pallas_call(
        functools.partial(choose_kernel, first),
        name="choose",
        out_shape=(out, out),
        in_specs=[pl.BlockSpec(memory_space=pltpu.SMEM), vmem],
        out_specs=(vmem, vmem),
        compiler_params=pltpu.CompilerParams(vmem_limit_bytes=24 * MB),
        cost_estimate=pl.CostEstimate(flops=0, bytes_accessed=10**6, transcendentals=0),
    )(send, p_tiles)


BLOCKS = 4


def local_kernel(
    col_ref, target_ref, p_hbm, a_ref, *refs
):
    part_refs, (left_ref, slot_ref, p_ref, packed, total, left, sem) = refs[:-7], refs[-7:]
    step = pl.program_id(0)
    blocks = p_ref.shape[0]
    slots = left_ref.shape[0] - 1
    spare = total.shape[0] - 1

    @pl.when(step == 0)
    def _():
        load = pltpu.make_async_copy(p_hbm, p_ref, sem.at[0])
        load.start()
        load.wait()

        @pl.loop(0, blocks)
        def _(i):
            packed[i] = column_pair(p_ref[i])

        @pl.loop(0, spare + 1)
        def _(i):
            total[i] = jnp.zeros(total.shape[1:], F32)

        @pl.loop(0, slots)
        def _(i):
            slot_ref[i] = -1

    neighbours = a_ref.shape[1]
    for i in range(BLOCKS):
        f = step * BLOCKS + i
        rows = row_pair(p_ref[f].T)
        places = []
        for k in range(neighbours):
            v = col_ref[f * neighbours + k]
            t = target_ref[f * neighbours + k]
            remote = v >= blocks
            slot = jnp.where(remote, v - blocks, slots)
            slot_ref[slot] = t
            places.append((slot, jnp.where(remote, 0, v), jnp.where(remote, spare, t)))
        lefts = [product(rows, column_pair(a_ref[i, k])) for k in range(neighbours)]
        for w, (slot, _, _) in zip(lefts, places):
            left[slot] = w
        terms = [product(row_pair(w), packed[q]) for w, (_, q, _) in zip(lefts, places)]
        for term, (_, _, t) in zip(terms, places):
            total[t] += term

    @pl.when(step == pl.num_programs(0) - 1)
    def _():
        stores = [pltpu.make_async_copy(left, left_ref, sem.at[len(part_refs)])]
        first = 0
        for i, part in enumerate(part_refs):
            stores.append(pltpu.make_async_copy(total.at[pl.ds(first, part.shape[0])], part, sem.at[i]))
            first += part.shape[0]
        for store in stores:
            store.start()
        for store in stores:
            store.wait()


def local_part(col, target, p_tiles, a_tiles, sizes, slots):
    blocks, bs, cw = p_tiles.shape
    neighbours = a_tiles.shape[1]
    parts = tuple(jax.ShapeDtypeStruct((size, cw, cw), F32) for size in sizes)
    left = jax.ShapeDtypeStruct((slots + 1, cw, bs), F32)
    return pl.pallas_call(
        local_kernel,
        name="local_part",
        grid_spec=pltpu.PrefetchScalarGridSpec(
            num_scalar_prefetch=2,
            grid=(blocks // BLOCKS,),
            in_specs=[
                pl.BlockSpec(memory_space=pltpu.HBM),
                pl.BlockSpec((BLOCKS, neighbours, bs, bs), lambda f, *_: (f, 0, 0, 0)),
            ],
            out_specs=(pl.BlockSpec(memory_space=pl.ANY),) * (len(parts) + 1)
            + (pl.BlockSpec(memory_space=pltpu.SMEM),),
            scratch_shapes=[
                pltpu.VMEM(p_tiles.shape, F32),
                pltpu.VMEM((blocks, 2 * bs, 2 * cw), BF16),
                pltpu.VMEM((sum(sizes) + 1, cw, cw), F32),
                pltpu.VMEM(left.shape, F32),
                pltpu.SemaphoreType.DMA((len(parts) + 1,)),
            ],
        ),
        out_shape=parts + (left, jax.ShapeDtypeStruct((slots + 8,), jnp.int32)),
        compiler_params=pltpu.CompilerParams(vmem_limit_bytes=28 * MB),
        cost_estimate=pl.CostEstimate(flops=10**9, bytes_accessed=10**7, transcendentals=0),
    )(col, target, p_tiles, a_tiles)


GROUP = 4


def remote_kernel(first, base, slot_ref, left_ref, lower_ref, upper_ref, *refs):
    parts, todo = refs[len(refs) // 2 : -1], refs[-1]
    capacity = lower_ref.shape[0]
    slots = (left_ref.shape[0] - 1) // 2
    places = 2 * capacity + GROUP
    held = sum(part.shape[0] for part in parts)

    def find(j, n):
        place = slot_ref[jnp.where(j < capacity, base + j, slots + base + j - capacity)] - first
        wanted = (place >= 0) & (place < held)
        todo[n] = j
        todo[n + places] = place
        return n + wanted.astype(jnp.int32)

    count = lax.fori_loop(0, 2 * capacity, find, jnp.int32(0))
    for i in range(GROUP):
        todo[count + i] = 0
        todo[count + i + places] = -1

    def step(g, carry):
        terms = []
        for i in range(GROUP):
            j = todo[g * GROUP + i]
            above = j >= capacity
            k = jnp.where(above, j - capacity, j)
            received = jnp.where(above, upper_ref[k], lower_ref[k])
            terms.append(product(row_pair(left_ref[base + k + jnp.where(above, slots, 0)]), column_pair(received)))
        for i, term in enumerate(terms):
            place = todo[g * GROUP + i + places]
            start = 0
            for part in parts:
                here = place - start

                @pl.when((here >= 0) & (here < part.shape[0]))
                def _():
                    part[here] += term

                start += part.shape[0]
        return carry

    lax.fori_loop(0, (count + GROUP - 1) // GROUP, step, 0)


def remote_part(first, base, slots, left, lower, upper, parts):
    n = len(parts)
    vmem = pl.BlockSpec(memory_space=pltpu.VMEM)
    return pl.pallas_call(
        functools.partial(remote_kernel, first, base),
        name="remote_part",
        out_shape=tuple(jax.ShapeDtypeStruct(part.shape, F32) for part in parts),
        in_specs=[pl.BlockSpec(memory_space=pltpu.SMEM)] + [vmem] * (3 + n),
        out_specs=(vmem,) * n,
        scratch_shapes=[pltpu.SMEM((4 * lower.shape[0] + 2 * GROUP,), jnp.int32)],
        input_output_aliases={4 + i: i for i in range(n)},
        compiler_params=pltpu.CompilerParams(vmem_limit_bytes=24 * MB),
        cost_estimate=pl.CostEstimate(flops=10**8, bytes_accessed=10**6, transcendentals=0),
    )(slots, left, lower, upper, *parts)


def place_kernel(pieces, *refs):
    n = len(pieces)
    ins = refs[:n]
    out_ref, held, load_sem, store_sem = refs[-4:]
    at = lax.axis_index("bulk")
    here = {"x": at // SIDE, "y": lax.rem(at, SIDE)}
    loads, stores = [], []
    first = 0
    for i, (ref, (where, axis, distance, stride)) in enumerate(zip(ins, pieces)):
        if axis is not None:
            where = where + lax.rem(here[axis] + distance, SIDE) * stride
        size = ref.shape[0]
        loads.append(pltpu.make_async_copy(ref, held.at[pl.ds(first, size)], load_sem.at[i]))
        stores.append(pltpu.make_async_copy(held.at[pl.ds(first, size)], out_ref.at[pl.ds(where, size)], store_sem.at[i]))
        first += size
    for load in loads:
        load.start()
    for load, store in zip(loads, stores):
        load.wait()
        store.start()
    for store in stores:
        store.wait()


def place(arrays, pieces, shape, out=None):
    anywhere = pl.BlockSpec(memory_space=pl.ANY)
    hbm = pl.BlockSpec(memory_space=pltpu.HBM)
    held = sum(array.shape[0] for array in arrays)
    args = list(arrays) + ([] if out is None else [out])
    return pl.pallas_call(
        functools.partial(place_kernel, pieces),
        name="place",
        out_shape=jax.ShapeDtypeStruct(shape, F32),
        in_specs=[anywhere] * len(arrays) + [hbm] * (len(args) - len(arrays)),
        out_specs=hbm,
        scratch_shapes=[
            pltpu.VMEM((held,) + shape[1:], F32),
            pltpu.SemaphoreType.DMA((len(arrays),)),
            pltpu.SemaphoreType.DMA((len(arrays),)),
        ],
        compiler_params=pltpu.CompilerParams(vmem_limit_bytes=16 * MB),
        input_output_aliases={} if out is None else {len(arrays): 0},
        cost_estimate=pl.CostEstimate(flops=0, bytes_accessed=2 * held * 65536, transcendentals=0),
    )(*args)


def route(dx, dy):
    pairs = []
    for x in range(SIDE):
        for y in range(SIDE):
            pairs.append((x * SIDE + y, (x + dx) % SIDE * SIDE + (y + dy) % SIDE))
    return pairs


def push(block, axis, distance):
    dx, dy = (distance, 0) if axis == "x" else (0, distance)
    return lax.ppermute(block, "bulk", route(dx, dy))


def swap(block, axis, odd):
    pairs = []
    for x in range(SIDE):
        for y in range(SIDE):
            to = [x, y]
            i = 0 if axis == "x" else 1
            to[i] = ((to[i] + odd) % SIDE ^ 1) - odd
            pairs.append((x * SIDE + y, to[0] % SIDE * SIDE + to[1] % SIDE))
    return lax.ppermute(block, "bulk", pairs)


def shifted(block, axis, distance):
    devices = range(lax.axis_size(axis))
    pairs = [(i - distance, i) for i in devices if i - distance in devices]
    return lax.ppermute(block, axis, pairs)


FIRST = 22
LANES = 2
LAYOUT = (6, 7, 4, 1, 0, 2, 3, 5)


def shards(p_tiles, a_tiles, col_ref, send_list, coarse_tile):
    tiles = 128
    e = tiles // (8 * LANES)
    mid = tiles // 2
    axes = (("x", "y"), ("y", "x")) * (LANES // 2)
    capacity = send_list.shape[2]
    at = lax.axis_index("bulk")
    lane = coarse_tile // (8 * e)
    shard = coarse_tile // (2 * e) % SIDE
    key = (shard - jnp.where(lane % 2 == 0, at // SIDE, at % SIDE)) % SIDE * 2 + coarse_tile // e % 2
    where = sum(jnp.where(key == i, at_eighth, 0) for i, at_eighth in enumerate(LAYOUT))
    target = ((where // 4 * LANES + lane) * 4 + where % 4) * e + coarse_tile % e

    halo = []
    for first, size in ((0, FIRST), (FIRST, capacity - FIRST)):
        to_lower, to_upper = choose(send_list[0], p_tiles, first, size)
        lower = shifted(to_upper, ("group", "bulk"), 1)
        upper = shifted(to_lower, ("group", "bulk"), -1)
        halo.append((lower, upper))
    early_sizes = [2 * e, 2 * e] * LANES
    late_sizes = [e, e, 2 * e] * LANES
    *parts, left, slot_tile = local_part(
        col_ref.reshape(-1), target.reshape(-1), p_tiles, a_tiles, early_sizes + late_sizes, 2 * capacity
    )
    early, late = parts[: len(early_sizes)], parts[len(early_sizes) :]
    early = remote_part(0, 0, slot_tile, left, *halo[0], early)
    late = remote_part(mid, 0, slot_tile, left, *halo[0], late)
    firsts = remote_part(0, FIRST, slot_tile, left, *halo[1], early)
    rests = remote_part(mid, FIRST, slot_tile, left, *halo[1], late)

    owned = []
    arrived = [
        (push(firsts[2 * h], axis, 1), push(firsts[2 * h + 1], axis, -1)) for h, (axis, _) in enumerate(axes)
    ]
    for h, (axis, _) in enumerate(axes):
        up, down, kept = rests[3 * h : 3 * h + 3]
        from_below, from_above = arrived[h]
        up = push(up + from_below[:e], axis, 1)
        down = push(down + from_above[:e], axis, -1)
        owned.append((kept[:e] + from_above[e:] + up, kept[e:] + from_below[e:] + down))
    gathered = []
    for h, (_, axis) in enumerate(axes):
        one, two = owned[h]
        one, two = one + swap(one, axis, 0), two + swap(two, axis, 1)
        one, two = one + swap(one, axis, 1), two + swap(two, axis, 0)
        gathered.append(jnp.concatenate([one, two]))
    first, first_pieces, last, last_pieces = [], [], [], []
    for h, (axis, _) in enumerate(axes):
        behind = push(gathered[h], axis, 1)
        ahead = push(gathered[h], axis, -1)
        far_one = push(behind[:e], axis, 1)
        far_two = push(ahead[e:], axis, -1)
        first += [gathered[h], behind, ahead]
        first_pieces += [(8 * h * e, axis, distance, 2 * e) for distance in (0, 3, 1)]
        last += [far_one, far_two]
        last_pieces += [(8 * h * e + side * e, axis, 2, 2 * e) for side in range(2)]
    shape = (tiles,) + p_tiles.shape[2:] * 2
    out = place(first, first_pieces, shape)
    return place(last, last_pieces, shape, out)


def solution(mesh):
    in_specs = (
        P(("group", "bulk"), None, None),
        P(("group", "bulk"), None, None, None),
        P(("group", "bulk"), None),
        P(("group", "bulk"), None, None),
        P(("group", "bulk"), None),
    )
    out_specs = P("group", None, None)
    return jax.shard_map(shards, mesh=mesh, in_specs=in_specs, out_specs=out_specs, check_vma=False)
```

```python
import functools

import jax
import jax.numpy as jnp
from jax import lax
from jax.experimental import pallas as pl
from jax.experimental.pallas import tpu as pltpu
from jax.sharding import PartitionSpec as P

F32 = jnp.float32
BF16 = jnp.bfloat16
SIDE = 4
MB = 1 << 20


def parts_of(x):
    high = x.astype(BF16)
    return high, (x - high.astype(F32)).astype(BF16)


def row_pair(x):
    return jnp.concatenate(parts_of(x), axis=1)


def column_pair(x):
    pair = row_pair(x)
    return jnp.concatenate([pair, pair], axis=0)


def fold(x):
    n = x.shape[1] // 2
    return x[:, :n] + x[:, n:]


def product(left_pair, right_pair):
    return fold(jnp.dot(left_pair, right_pair, preferred_element_type=F32))


def choose_kernel(first, send_ref, p_ref, low_ref, up_ref, sem):
    outs = (low_ref, up_ref)
    for j in range(low_ref.shape[0]):
        for side, out in enumerate(outs):
            tile = jnp.maximum(send_ref[side, first + j], 0)
            pltpu.make_async_copy(p_ref.at[tile], out.at[j], sem.at[side]).start()
    for side, out in enumerate(outs):
        pltpu.make_async_copy(p_ref.at[pl.ds(0, out.shape[0])], out, sem.at[side]).wait()


def choose(send, p_tiles, first, size):
    out = jax.ShapeDtypeStruct((size,) + p_tiles.shape[1:], F32)
    vmem = pl.BlockSpec(memory_space=pltpu.VMEM)
    return pl.pallas_call(
        functools.partial(choose_kernel, first),
        name="choose",
        out_shape=(out, out),
        in_specs=[pl.BlockSpec(memory_space=pltpu.SMEM), pl.BlockSpec(memory_space=pl.ANY)],
        out_specs=(vmem, vmem),
        scratch_shapes=[pltpu.SemaphoreType.DMA((2,))],
        compiler_params=pltpu.CompilerParams(vmem_limit_bytes=58 * MB),
        cost_estimate=pl.CostEstimate(flops=0, bytes_accessed=10**6, transcendentals=0),
    )(send, p_tiles)


BLOCKS = 4


def local_kernel(
    col_ref, target_ref, p_hbm, a_ref, *refs
):
    part_refs, (left_ref, slot_ref, p_ref, packed, total, left, sem) = refs[:-7], refs[-7:]
    step = pl.program_id(0)
    blocks = p_ref.shape[0]
    slots = left_ref.shape[0] - 1
    spare = total.shape[0] - 1

    @pl.when(step == 0)
    def _():
        load = pltpu.make_async_copy(p_hbm, p_ref, sem.at[0])
        load.start()
        load.wait()

        @pl.loop(0, blocks)
        def _(i):
            packed[i] = column_pair(p_ref[i])

        @pl.loop(0, spare + 1)
        def _(i):
            total[i] = jnp.zeros(total.shape[1:], F32)

        @pl.loop(0, slots)
        def _(i):
            slot_ref[i] = -1

    neighbours = a_ref.shape[1]
    for i in range(BLOCKS):
        f = step * BLOCKS + i
        rows = row_pair(p_ref[f].T)
        places = []
        for k in range(neighbours):
            v = col_ref[f * neighbours + k]
            t = target_ref[f * neighbours + k]
            remote = v >= blocks
            slot = jnp.where(remote, v - blocks, slots)
            slot_ref[slot] = t
            places.append((slot, jnp.where(remote, 0, v), jnp.where(remote, spare, t)))
        lefts = [product(rows, column_pair(a_ref[i, k])) for k in range(neighbours)]
        for w, (slot, _, _) in zip(lefts, places):
            left[slot] = w
        terms = [product(row_pair(w), packed[q]) for w, (_, q, _) in zip(lefts, places)]
        for term, (_, _, t) in zip(terms, places):
            total[t] += term

    @pl.when(step == pl.num_programs(0) - 1)
    def _():
        stores = [pltpu.make_async_copy(left, left_ref, sem.at[len(part_refs)])]
        first = 0
        for i, part in enumerate(part_refs):
            stores.append(pltpu.make_async_copy(total.at[pl.ds(first, part.shape[0])], part, sem.at[i]))
            first += part.shape[0]
        for store in stores:
            store.start()
        for store in stores:
            store.wait()


def local_part(col, target, p_tiles, a_tiles, sizes, slots):
    blocks, bs, cw = p_tiles.shape
    neighbours = a_tiles.shape[1]
    parts = tuple(jax.ShapeDtypeStruct((size, cw, cw), F32) for size in sizes)
    left = jax.ShapeDtypeStruct((slots + 1, cw, bs), F32)
    return pl.pallas_call(
        local_kernel,
        name="local_part",
        grid_spec=pltpu.PrefetchScalarGridSpec(
            num_scalar_prefetch=2,
            grid=(blocks // BLOCKS,),
            in_specs=[
                pl.BlockSpec(memory_space=pltpu.HBM),
                pl.BlockSpec((BLOCKS, neighbours, bs, bs), lambda f, *_: (f, 0, 0, 0)),
            ],
            out_specs=(pl.BlockSpec(memory_space=pl.ANY),) * (len(parts) + 1)
            + (pl.BlockSpec(memory_space=pltpu.SMEM),),
            scratch_shapes=[
                pltpu.VMEM(p_tiles.shape, F32),
                pltpu.VMEM((blocks, 2 * bs, 2 * cw), BF16),
                pltpu.VMEM((sum(sizes) + 1, cw, cw), F32),
                pltpu.VMEM(left.shape, F32),
                pltpu.SemaphoreType.DMA((len(parts) + 1,)),
            ],
        ),
        out_shape=parts + (left, jax.ShapeDtypeStruct((slots + 8,), jnp.int32)),
        compiler_params=pltpu.CompilerParams(vmem_limit_bytes=28 * MB),
        cost_estimate=pl.CostEstimate(flops=10**9, bytes_accessed=10**7, transcendentals=0),
    )(col, target, p_tiles, a_tiles)


GROUP = 4


def remote_kernel(first, base, slot_ref, left_ref, lower_ref, upper_ref, *refs):
    parts, todo = refs[len(refs) // 2 : -1], refs[-1]
    capacity = lower_ref.shape[0]
    slots = (left_ref.shape[0] - 1) // 2
    places = 2 * capacity + GROUP
    held = sum(part.shape[0] for part in parts)

    def find(j, n):
        place = slot_ref[jnp.where(j < capacity, base + j, slots + base + j - capacity)] - first
        wanted = (place >= 0) & (place < held)
        todo[n] = j
        todo[n + places] = place
        return n + wanted.astype(jnp.int32)

    count = lax.fori_loop(0, 2 * capacity, find, jnp.int32(0))
    for i in range(GROUP):
        todo[count + i] = 0
        todo[count + i + places] = -1

    def step(g, carry):
        terms = []
        for i in range(GROUP):
            j = todo[g * GROUP + i]
            above = j >= capacity
            k = jnp.where(above, j - capacity, j)
            received = jnp.where(above, upper_ref[k], lower_ref[k])
            terms.append(product(row_pair(left_ref[base + k + jnp.where(above, slots, 0)]), column_pair(received)))
        for i, term in enumerate(terms):
            place = todo[g * GROUP + i + places]
            start = 0
            for part in parts:
                here = place - start

                @pl.when((here >= 0) & (here < part.shape[0]))
                def _():
                    part[here] += term

                start += part.shape[0]
        return carry

    lax.fori_loop(0, (count + GROUP - 1) // GROUP, step, 0)


def remote_part(first, base, slots, left, lower, upper, parts):
    n = len(parts)
    vmem = pl.BlockSpec(memory_space=pltpu.VMEM)
    return pl.pallas_call(
        functools.partial(remote_kernel, first, base),
        name="remote_part",
        out_shape=tuple(jax.ShapeDtypeStruct(part.shape, F32) for part in parts),
        in_specs=[pl.BlockSpec(memory_space=pltpu.SMEM)] + [vmem] * (3 + n),
        out_specs=(vmem,) * n,
        scratch_shapes=[pltpu.SMEM((4 * lower.shape[0] + 2 * GROUP,), jnp.int32)],
        input_output_aliases={4 + i: i for i in range(n)},
        compiler_params=pltpu.CompilerParams(vmem_limit_bytes=24 * MB),
        cost_estimate=pl.CostEstimate(flops=10**8, bytes_accessed=10**6, transcendentals=0),
    )(slots, left, lower, upper, *parts)


def place_kernel(pieces, *refs):
    n = len(pieces)
    ins = refs[:n]
    out_ref, held, load_sem, store_sem = refs[-4:]
    at = lax.axis_index("bulk")
    here = {"x": at // SIDE, "y": lax.rem(at, SIDE)}
    loads, stores = [], []
    first = 0
    for i, (ref, (where, axis, distance, stride)) in enumerate(zip(ins, pieces)):
        if axis is not None:
            where = where + lax.rem(here[axis] + distance, SIDE) * stride
        size = ref.shape[0]
        loads.append(pltpu.make_async_copy(ref, held.at[pl.ds(first, size)], load_sem.at[i]))
        stores.append(pltpu.make_async_copy(held.at[pl.ds(first, size)], out_ref.at[pl.ds(where, size)], store_sem.at[i]))
        first += size
    for load in loads:
        load.start()
    for load, store in zip(loads, stores):
        load.wait()
        store.start()
    for store in stores:
        store.wait()


def place(arrays, pieces, shape, out=None):
    anywhere = pl.BlockSpec(memory_space=pl.ANY)
    hbm = pl.BlockSpec(memory_space=pltpu.HBM)
    held = sum(array.shape[0] for array in arrays)
    args = list(arrays) + ([] if out is None else [out])
    return pl.pallas_call(
        functools.partial(place_kernel, pieces),
        name="place",
        out_shape=jax.ShapeDtypeStruct(shape, F32),
        in_specs=[anywhere] * len(arrays) + [hbm] * (len(args) - len(arrays)),
        out_specs=hbm,
        scratch_shapes=[
            pltpu.VMEM((held,) + shape[1:], F32),
            pltpu.SemaphoreType.DMA((len(arrays),)),
            pltpu.SemaphoreType.DMA((len(arrays),)),
        ],
        compiler_params=pltpu.CompilerParams(vmem_limit_bytes=16 * MB),
        input_output_aliases={} if out is None else {len(arrays): 0},
        cost_estimate=pl.CostEstimate(flops=0, bytes_accessed=2 * held * 65536, transcendentals=0),
    )(*args)


def route(dx, dy):
    pairs = []
    for x in range(SIDE):
        for y in range(SIDE):
            pairs.append((x * SIDE + y, (x + dx) % SIDE * SIDE + (y + dy) % SIDE))
    return pairs


def push(block, axis, distance):
    dx, dy = (distance, 0) if axis == "x" else (0, distance)
    return lax.ppermute(block, "bulk", route(dx, dy))


def swap(block, axis, odd):
    pairs = []
    for x in range(SIDE):
        for y in range(SIDE):
            to = [x, y]
            i = 0 if axis == "x" else 1
            to[i] = ((to[i] + odd) % SIDE ^ 1) - odd
            pairs.append((x * SIDE + y, to[0] % SIDE * SIDE + to[1] % SIDE))
    return lax.ppermute(block, "bulk", pairs)


def shifted(block, axis, distance):
    devices = range(lax.axis_size(axis))
    pairs = [(i - distance, i) for i in devices if i - distance in devices]
    return lax.ppermute(block, axis, pairs)


FIRST = 20
LANES = 2
LAYOUT = (6, 7, 4, 1, 0, 2, 3, 5)


def shards(p_tiles, a_tiles, col_ref, send_list, coarse_tile):
    tiles = 128
    e = tiles // (8 * LANES)
    mid = tiles // 2
    axes = (("x", "y"), ("y", "x")) * (LANES // 2)
    capacity = send_list.shape[2]
    at = lax.axis_index("bulk")
    lane = coarse_tile // (8 * e)
    shard = coarse_tile // (2 * e) % SIDE
    key = (shard - jnp.where(lane % 2 == 0, at // SIDE, at % SIDE)) % SIDE * 2 + coarse_tile // e % 2
    where = sum(jnp.where(key == i, at_eighth, 0) for i, at_eighth in enumerate(LAYOUT))
    target = ((where // 4 * LANES + lane) * 4 + where % 4) * e + coarse_tile % e

    halo = []
    for first, size in ((0, FIRST), (FIRST, capacity - FIRST)):
        to_lower, to_upper = choose(send_list[0], p_tiles, first, size)
        lower = shifted(to_upper, ("group", "bulk"), 1)
        upper = shifted(to_lower, ("group", "bulk"), -1)
        halo.append((lower, upper))
    early_sizes = [2 * e, 2 * e] * LANES
    late_sizes = [e, e, 2 * e] * LANES
    *parts, left, slot_tile = local_part(
        col_ref.reshape(-1), target.reshape(-1), p_tiles, a_tiles, early_sizes + late_sizes, 2 * capacity
    )
    early, late = parts[: len(early_sizes)], parts[len(early_sizes) :]
    early = remote_part(0, 0, slot_tile, left, *halo[0], early)
    late = remote_part(mid, 0, slot_tile, left, *halo[0], late)
    firsts = remote_part(0, FIRST, slot_tile, left, *halo[1], early)
    rests = remote_part(mid, FIRST, slot_tile, left, *halo[1], late)

    owned = []
    arrived = [
        (push(firsts[2 * h], axis, 1), push(firsts[2 * h + 1], axis, -1)) for h, (axis, _) in enumerate(axes)
    ]
    for h, (axis, _) in enumerate(axes):
        up, down, kept = rests[3 * h : 3 * h + 3]
        from_below, from_above = arrived[h]
        up = push(up + from_below[:e], axis, 1)
        down = push(down + from_above[:e], axis, -1)
        owned.append((kept[:e] + from_above[e:] + up, kept[e:] + from_below[e:] + down))
    gathered = []
    for h, (_, axis) in enumerate(axes):
        one, two = owned[h]
        one, two = one + swap(one, axis, 0), two + swap(two, axis, 1)
        one, two = one + swap(one, axis, 1), two + swap(two, axis, 0)
        gathered.append(jnp.concatenate([one, two]))
    first, first_pieces, last, last_pieces = [], [], [], []
    for h, (axis, _) in enumerate(axes):
        behind = push(gathered[h], axis, 1)
        ahead = push(gathered[h], axis, -1)
        far_one = push(behind[:e], axis, 1)
        far_two = push(ahead[e:], axis, -1)
        first += [gathered[h], behind, ahead]
        first_pieces += [(8 * h * e, axis, distance, 2 * e) for distance in (0, 3, 1)]
        last += [far_one, far_two]
        last_pieces += [(8 * h * e + side * e, axis, 2, 2 * e) for side in range(2)]
    shape = (tiles,) + p_tiles.shape[2:] * 2
    out = place(first, first_pieces, shape)
    return place(last, last_pieces, shape, out)


def solution(mesh):
    in_specs = (
        P(("group", "bulk"), None, None),
        P(("group", "bulk"), None, None, None),
        P(("group", "bulk"), None),
        P(("group", "bulk"), None, None),
        P(("group", "bulk"), None),
    )
    out_specs = P("group", None, None)
    return jax.shard_map(shards, mesh=mesh, in_specs=in_specs, out_specs=out_specs, check_vma=False)
```

```python
import functools

import jax
import jax.numpy as jnp
from jax import lax
from jax.experimental import pallas as pl
from jax.experimental.pallas import tpu as pltpu
from jax.sharding import PartitionSpec as P

F32 = jnp.float32
BF16 = jnp.bfloat16
SIDE = 4
MB = 1 << 20


def parts_of(x):
    high = x.astype(BF16)
    return high, (x - high.astype(F32)).astype(BF16)


def row_pair(x):
    return jnp.concatenate(parts_of(x), axis=1)


def column_pair(x):
    pair = row_pair(x)
    return jnp.concatenate([pair, pair], axis=0)


def fold(x):
    n = x.shape[1] // 2
    return x[:, :n] + x[:, n:]


def product(left_pair, right_pair):
    return fold(jnp.dot(left_pair, right_pair, preferred_element_type=F32))


def choose_kernel(first, send_ref, p_ref, low_ref, up_ref, sem):
    outs = (low_ref, up_ref)
    for j in range(low_ref.shape[0]):
        for side, out in enumerate(outs):
            tile = jnp.maximum(send_ref[side, first + j], 0)
            pltpu.make_async_copy(p_ref.at[tile], out.at[j], sem.at[side]).start()
    for side, out in enumerate(outs):
        pltpu.make_async_copy(p_ref.at[pl.ds(0, out.shape[0])], out, sem.at[side]).wait()


def choose(send, p_tiles, first, size):
    out = jax.ShapeDtypeStruct((size,) + p_tiles.shape[1:], F32)
    vmem = pl.BlockSpec(memory_space=pltpu.VMEM)
    return pl.pallas_call(
        functools.partial(choose_kernel, first),
        name="choose",
        out_shape=(out, out),
        in_specs=[pl.BlockSpec(memory_space=pltpu.SMEM), pl.BlockSpec(memory_space=pl.ANY)],
        out_specs=(vmem, vmem),
        scratch_shapes=[pltpu.SemaphoreType.DMA((2,))],
        compiler_params=pltpu.CompilerParams(vmem_limit_bytes=58 * MB),
        cost_estimate=pl.CostEstimate(flops=0, bytes_accessed=10**6, transcendentals=0),
    )(send, p_tiles)


BLOCKS = 4


def local_kernel(
    col_ref, target_ref, p_hbm, a_ref, *refs
):
    part_refs, (left_ref, slot_ref, p_ref, packed, total, left, sem) = refs[:-7], refs[-7:]
    step = pl.program_id(0)
    blocks = p_ref.shape[0]
    slots = left_ref.shape[0] - 1
    spare = total.shape[0] - 1

    @pl.when(step == 0)
    def _():
        load = pltpu.make_async_copy(p_hbm, p_ref, sem.at[0])
        load.start()
        load.wait()

        @pl.loop(0, blocks)
        def _(i):
            packed[i] = column_pair(p_ref[i])

        @pl.loop(0, spare + 1)
        def _(i):
            total[i] = jnp.zeros(total.shape[1:], F32)

        @pl.loop(0, slots)
        def _(i):
            slot_ref[i] = -1

    neighbours = a_ref.shape[1]
    for i in range(BLOCKS):
        f = step * BLOCKS + i
        rows = row_pair(p_ref[f].T)
        places = []
        for k in range(neighbours):
            v = col_ref[f * neighbours + k]
            t = target_ref[f * neighbours + k]
            remote = v >= blocks
            slot = jnp.where(remote, v - blocks, slots)
            slot_ref[slot] = t
            places.append((slot, jnp.where(remote, 0, v), jnp.where(remote, spare, t)))
        lefts = [product(rows, column_pair(a_ref[i, k])) for k in range(neighbours)]
        for w, (slot, _, _) in zip(lefts, places):
            left[slot] = w
        terms = [product(row_pair(w), packed[q]) for w, (_, q, _) in zip(lefts, places)]
        for term, (_, _, t) in zip(terms, places):
            total[t] += term

    @pl.when(step == pl.num_programs(0) - 1)
    def _():
        stores = [pltpu.make_async_copy(left, left_ref, sem.at[len(part_refs)])]
        first = 0
        for i, part in enumerate(part_refs):
            stores.append(pltpu.make_async_copy(total.at[pl.ds(first, part.shape[0])], part, sem.at[i]))
            first += part.shape[0]
        for store in stores:
            store.start()
        for store in stores:
            store.wait()


def local_part(col, target, p_tiles, a_tiles, sizes, slots):
    blocks, bs, cw = p_tiles.shape
    neighbours = a_tiles.shape[1]
    parts = tuple(jax.ShapeDtypeStruct((size, cw, cw), F32) for size in sizes)
    left = jax.ShapeDtypeStruct((slots + 1, cw, bs), F32)
    return pl.pallas_call(
        local_kernel,
        name="local_part",
        grid_spec=pltpu.PrefetchScalarGridSpec(
            num_scalar_prefetch=2,
            grid=(blocks // BLOCKS,),
            in_specs=[
                pl.BlockSpec(memory_space=pltpu.HBM),
                pl.BlockSpec((BLOCKS, neighbours, bs, bs), lambda f, *_: (f, 0, 0, 0)),
            ],
            out_specs=(pl.BlockSpec(memory_space=pl.ANY),) * (len(parts) + 1)
            + (pl.BlockSpec(memory_space=pltpu.SMEM),),
            scratch_shapes=[
                pltpu.VMEM(p_tiles.shape, F32),
                pltpu.VMEM((blocks, 2 * bs, 2 * cw), BF16),
                pltpu.VMEM((sum(sizes) + 1, cw, cw), F32),
                pltpu.VMEM(left.shape, F32),
                pltpu.SemaphoreType.DMA((len(parts) + 1,)),
            ],
        ),
        out_shape=parts + (left, jax.ShapeDtypeStruct((slots + 8,), jnp.int32)),
        compiler_params=pltpu.CompilerParams(vmem_limit_bytes=28 * MB),
        cost_estimate=pl.CostEstimate(flops=10**9, bytes_accessed=10**7, transcendentals=0),
    )(col, target, p_tiles, a_tiles)


GROUP = 4


def remote_kernel(first, base, slot_ref, left_ref, received_ref, *refs):
    parts, todo = refs[len(refs) // 2 : -1], refs[-1]
    capacity = received_ref.shape[0]
    places = capacity + GROUP
    held = sum(part.shape[0] for part in parts)

    def find(j, n):
        place = slot_ref[base + j] - first
        wanted = (place >= 0) & (place < held)
        todo[n] = j
        todo[n + places] = place
        return n + wanted.astype(jnp.int32)

    count = lax.fori_loop(0, capacity, find, jnp.int32(0))
    for i in range(GROUP):
        todo[count + i] = 0
        todo[count + i + places] = -1

    def step(g, carry):
        terms = []
        for i in range(GROUP):
            j = todo[g * GROUP + i]
            terms.append(product(row_pair(left_ref[base + j]), column_pair(received_ref[j])))
        for i, term in enumerate(terms):
            place = todo[g * GROUP + i + places]
            start = 0
            for part in parts:
                here = place - start

                @pl.when((here >= 0) & (here < part.shape[0]))
                def _():
                    part[here] += term

                start += part.shape[0]
        return carry

    lax.fori_loop(0, (count + GROUP - 1) // GROUP, step, 0)


def remote_part(first, base, slots, left, received, parts):
    n = len(parts)
    vmem = pl.BlockSpec(memory_space=pltpu.VMEM)
    return pl.pallas_call(
        functools.partial(remote_kernel, first, base),
        name="remote_part",
        out_shape=tuple(jax.ShapeDtypeStruct(part.shape, F32) for part in parts),
        in_specs=[pl.BlockSpec(memory_space=pltpu.SMEM)] + [vmem] * (2 + n),
        out_specs=(vmem,) * n,
        scratch_shapes=[pltpu.SMEM((2 * received.shape[0] + 2 * GROUP,), jnp.int32)],
        input_output_aliases={3 + i: i for i in range(n)},
        compiler_params=pltpu.CompilerParams(vmem_limit_bytes=24 * MB),
        cost_estimate=pl.CostEstimate(flops=10**8, bytes_accessed=10**6, transcendentals=0),
    )(slots, left, received, *parts)


def place_kernel(pieces, *refs):
    n = len(pieces)
    ins = refs[:n]
    out_ref, held, load_sem, store_sem = refs[-4:]
    at = lax.axis_index("bulk")
    here = {"x": at // SIDE, "y": lax.rem(at, SIDE)}
    loads, stores = [], []
    first = 0
    for i, (ref, (where, axis, distance, stride)) in enumerate(zip(ins, pieces)):
        if axis is not None:
            where = where + lax.rem(here[axis] + distance, SIDE) * stride
        size = ref.shape[0]
        loads.append(pltpu.make_async_copy(ref, held.at[pl.ds(first, size)], load_sem.at[i]))
        stores.append(pltpu.make_async_copy(held.at[pl.ds(first, size)], out_ref.at[pl.ds(where, size)], store_sem.at[i]))
        first += size
    for load in loads:
        load.start()
    for load, store in zip(loads, stores):
        load.wait()
        store.start()
    for store in stores:
        store.wait()


def place(arrays, pieces, shape, out=None):
    anywhere = pl.BlockSpec(memory_space=pl.ANY)
    hbm = pl.BlockSpec(memory_space=pltpu.HBM)
    held = sum(array.shape[0] for array in arrays)
    args = list(arrays) + ([] if out is None else [out])
    return pl.pallas_call(
        functools.partial(place_kernel, pieces),
        name="place",
        out_shape=jax.ShapeDtypeStruct(shape, F32),
        in_specs=[anywhere] * len(arrays) + [hbm] * (len(args) - len(arrays)),
        out_specs=hbm,
        scratch_shapes=[
            pltpu.VMEM((held,) + shape[1:], F32),
            pltpu.SemaphoreType.DMA((len(arrays),)),
            pltpu.SemaphoreType.DMA((len(arrays),)),
        ],
        compiler_params=pltpu.CompilerParams(vmem_limit_bytes=16 * MB),
        input_output_aliases={} if out is None else {len(arrays): 0},
        cost_estimate=pl.CostEstimate(flops=0, bytes_accessed=2 * held * 65536, transcendentals=0),
    )(*args)


def route(dx, dy):
    pairs = []
    for x in range(SIDE):
        for y in range(SIDE):
            pairs.append((x * SIDE + y, (x + dx) % SIDE * SIDE + (y + dy) % SIDE))
    return pairs


def push(block, axis, distance):
    dx, dy = (distance, 0) if axis == "x" else (0, distance)
    return lax.ppermute(block, "bulk", route(dx, dy))


def swap(block, axis, odd):
    pairs = []
    for x in range(SIDE):
        for y in range(SIDE):
            to = [x, y]
            i = 0 if axis == "x" else 1
            to[i] = ((to[i] + odd) % SIDE ^ 1) - odd
            pairs.append((x * SIDE + y, to[0] % SIDE * SIDE + to[1] % SIDE))
    return lax.ppermute(block, "bulk", pairs)


def shifted(block, axis, distance):
    devices = range(lax.axis_size(axis))
    pairs = [(i - distance, i) for i in devices if i - distance in devices]
    return lax.ppermute(block, axis, pairs)


FIRST = 20
LANES = 2
LAYOUT = (6, 7, 4, 1, 0, 2, 3, 5)


def shards(p_tiles, a_tiles, col_ref, send_list, coarse_tile):
    tiles = 128
    e = tiles // (8 * LANES)
    mid = tiles // 2
    axes = (("x", "y"), ("y", "x")) * (LANES // 2)
    capacity = send_list.shape[2]
    at = lax.axis_index("bulk")
    lane = coarse_tile // (8 * e)
    shard = coarse_tile // (2 * e) % SIDE
    key = (shard - jnp.where(lane % 2 == 0, at // SIDE, at % SIDE)) % SIDE * 2 + coarse_tile // e % 2
    where = sum(jnp.where(key == i, at_eighth, 0) for i, at_eighth in enumerate(LAYOUT))
    target = ((where // 4 * LANES + lane) * 4 + where % 4) * e + coarse_tile % e

    halo = []
    for first, size in ((0, FIRST), (FIRST, capacity - FIRST)):
        to_lower, to_upper = choose(send_list[0], p_tiles, first, size)
        lower = shifted(to_upper, ("group", "bulk"), 1)
        upper = shifted(to_lower, ("group", "bulk"), -1)
        halo.append((lower, upper))
    early_sizes = [2 * e, 2 * e] * LANES
    late_sizes = [e, e, 2 * e] * LANES
    *parts, left, slot_tile = local_part(
        col_ref.reshape(-1), target.reshape(-1), p_tiles, a_tiles, early_sizes + late_sizes, 2 * capacity
    )
    early, late = parts[: len(early_sizes)], parts[len(early_sizes) :]
    firsts, rests = early, late
    for base, received in ((0, halo[0]), (FIRST, halo[1])):
        for side, tiles_in in enumerate(received):
            firsts = remote_part(0, side * capacity + base, slot_tile, left, tiles_in, firsts)
            rests = remote_part(mid, side * capacity + base, slot_tile, left, tiles_in, rests)

    owned = []
    arrived = [
        (push(firsts[2 * h], axis, 1), push(firsts[2 * h + 1], axis, -1)) for h, (axis, _) in enumerate(axes)
    ]
    for h, (axis, _) in enumerate(axes):
        up, down, kept = rests[3 * h : 3 * h + 3]
        from_below, from_above = arrived[h]
        up = push(up + from_below[:e], axis, 1)
        down = push(down + from_above[:e], axis, -1)
        owned.append((kept[:e] + from_above[e:] + up, kept[e:] + from_below[e:] + down))
    gathered = []
    for h, (_, axis) in enumerate(axes):
        one, two = owned[h]
        one, two = one + swap(one, axis, 0), two + swap(two, axis, 1)
        one, two = one + swap(one, axis, 1), two + swap(two, axis, 0)
        gathered.append(jnp.concatenate([one, two]))
    first, first_pieces, last, last_pieces = [], [], [], []
    for h, (axis, _) in enumerate(axes):
        behind = push(gathered[h], axis, 1)
        ahead = push(gathered[h], axis, -1)
        far_one = push(behind[:e], axis, 1)
        far_two = push(ahead[e:], axis, -1)
        first += [gathered[h], behind, ahead]
        first_pieces += [(8 * h * e, axis, distance, 2 * e) for distance in (0, 3, 1)]
        last += [far_one, far_two]
        last_pieces += [(8 * h * e + side * e, axis, 2, 2 * e) for side in range(2)]
    shape = (tiles,) + p_tiles.shape[2:] * 2
    out = place(first, first_pieces, shape)
    return place(last, last_pieces, shape, out)


def solution(mesh):
    in_specs = (
        P(("group", "bulk"), None, None),
        P(("group", "bulk"), None, None, None),
        P(("group", "bulk"), None),
        P(("group", "bulk"), None, None),
        P(("group", "bulk"), None),
    )
    out_specs = P("group", None, None)
    return jax.shard_map(shards, mesh=mesh, in_specs=in_specs, out_specs=out_specs, check_vma=False)
```
